32 devices in a mesh: groups: 2 (over y), lists: 8 (over z, x), sub: 2 (over core).
Axes of the slice: x: 2, y: 2, z: 4, core: 2. Of those that a mesh axis runs over, the one named last changes fastest.
Arguments:
- tokens: bfloat16 [3072, 8, 1024], P(('groups', 'lists', 'sub')), parts along dimension 0, may hold values from -6 to 6
- w_in: bfloat16 [1024, 2048], replicated, may hold values from -0.1875 to 0.1875
- w_out: bfloat16 [2048, 1024], replicated, may hold values from -0.125 to 0.125
- gain: float32 [1024], replicated, may hold values from 0.1 to 1.9
- centroids: bfloat16 [65536, 1024], P(('lists', 'sub')), may hold values from -6 to 6
- list_slot: int32 [131072], P('groups'), parts along dimension 0, may hold values from 0 to 65535, as said below
- assign: int32 [3072], P(('groups', 'lists', 'sub')), parts along dimension 0, may hold values from 0 to 65535, as said below
- codes: int32 [3072, 64], P(('groups', 'lists', 'sub')), parts along dimension 0, may hold values from 0 to 255, as said below
- list_weight: float32 [131072], P('groups'), parts along dimension 0, may hold values from 0.25 to 4
Outputs:
- updated_centroids: bfloat16 [131072, 1024], P(('groups', 'lists', 'sub')), parts along dimension 0
- codewords: float32 [512, 1024], P(('groups', 'lists', 'sub')), parts along dimension 0
The draws below stay inside these ranges and needn't reach their ends.
There are 2 independent parts, one for each index of `groups`. The reference program is written for one: setup_inputs(seed, part) draws one part's arguments, and reference() takes and returns one part's arrays. A program takes and returns all parts, laid end to end along the dimension named above; an argument that names none is the same for every part. Nothing has to cross between parts.
Inputs may be any that keep to these rules, and one draw needn't show every extreme that they name: In every aligned block of 96 passages, at most 12 have slots list_slot[assign] within one device's block of 4096 slots, and in every block some device's slots take exactly 12. In every aligned block of 96 passages, at most 768 of its codes name codewords within one device's block of codewords, and in every block some device's codewords take exactly 768. `list_slot`: each slot once.
All inputs are finite; a program needn't handle non-finite values.
Results may differ from the reference program's by a relative error of at most 0.0023.
Values may be sent and summed in bfloat16 or wider, within the bound.
A program may use at most 128 MiB of HBM per device.

```python
import math
import jax
import jax.numpy as jnp
from jax import lax

D = 1024
FF_WIN = 2048
M = 64
CODES = 256
LISTS = 65536
LEN = 8
P_DEV = 96
PASSAGES = 1536
LISTS_DEV = 4096
ROW_CAP = 12
PIECE_CAP = 768
N_LISTS = 8
N_SUB = 2


def slot_table(key):
    return jax.random.permutation(jax.random.fold_in(key, 101), LISTS).astype(jnp.int32)


def capped_owners(key, rows, devices, limit):
    first_key, second_key, third_key = jax.random.split(key, 3)
    order = jax.random.permutation(first_key, devices).astype(jnp.int32)
    others = jnp.repeat(order[1:], limit, total_repeat_length=(devices - 1) * limit)
    others = jax.random.permutation(second_key, others)
    leading = jnp.full((limit,), 1, jnp.int32) * order[0]
    sequence = jnp.concatenate([leading, others])[:rows]
    return jax.random.permutation(third_key, sequence).astype(jnp.int32)


def draw_list_slot(key, part):
    return slot_table(key)


def draw_assign(key, part):
    table = slot_table(key)
    inverse = jnp.argsort(table).astype(jnp.int32)
    key = jax.random.fold_in(key, 7)
    devices = N_LISTS * N_SUB
    keys = jax.random.split(key, devices)
    owners = jax.vmap(lambda one_key: capped_owners(one_key, P_DEV, devices, ROW_CAP))(keys)
    offset = jax.random.randint(jax.random.fold_in(key, 9), (devices, P_DEV), 0, LISTS_DEV).astype(jnp.int32)
    slots = owners * LISTS_DEV + offset
    return jnp.take(inverse, slots.reshape(devices * P_DEV)).astype(jnp.int32)


def draw_codes(key, part):
    key = jax.random.fold_in(key, 13)
    devices = N_LISTS * N_SUB
    held = CODES // devices
    keys = jax.random.split(key, devices)
    owners = jax.vmap(lambda one_key: capped_owners(one_key, P_DEV * M, devices, PIECE_CAP))(keys)
    within = jax.random.randint(jax.random.fold_in(key, 17), (devices, P_DEV * M), 0, held).astype(jnp.int32)
    return (owners * held + within).reshape(devices * P_DEV, M).astype(jnp.int32)


def level_of(rng, extent, cuts, smallest, top_value):
    loudness, own = 1.0, jax.random.fold_in(rng, 6)
    for axis_at, blocks in cuts:
        heights = jnp.exp(jax.random.uniform(jax.random.fold_in(own, axis_at), (blocks,), jnp.float32, smallest / len(cuts), top_value / len(cuts)))
        loudness = loudness * jnp.repeat(heights, extent[axis_at] // blocks).reshape([-1 if axis == axis_at else 1 for axis in range(len(extent))])
    return loudness


def normal_values(own_key, shape, scale, most, cuts=(), kind=jnp.bfloat16):
    entries = jax.random.normal(own_key, shape, jnp.float32) * scale
    if len(cuts) > 0:
        entries = level_of(own_key, shape, cuts, -0.22, 0.18) * entries
    return jnp.clip(entries, min=-most, max=most).astype(kind)


def setup_inputs(seed: int = 0, part: int = 0) -> dict:
    key_of = jax.random.split(jax.random.key(seed), 10)
    own_keys = jax.random.split(jax.random.fold_in(key_of[9], part), 10)
    return {
        "tokens": normal_values(own_keys[0], (PASSAGES, LEN, D), 1.0, 6.0, ((0, 16),)),
        "w_in": normal_values(key_of[1], (D, FF_WIN), D ** -0.5, 0.1875),
        "w_out": normal_values(key_of[2], (FF_WIN, D), FF_WIN ** -0.5, 0.125),
        "gain": jnp.clip(1.0 + 0.18 * jax.random.normal(key_of[3], (D,), jnp.float32), 0.1, 1.9),
        "centroids": normal_values(key_of[4], (LISTS, D), 1.0, 6.0, ((0, 16),)),
        "list_slot": draw_list_slot(jax.random.fold_in(jax.random.fold_in(key_of[9], part), 71), part),
        "assign": draw_assign(jax.random.fold_in(jax.random.fold_in(key_of[9], part), 71), part),
        "codes": draw_codes(jax.random.fold_in(jax.random.fold_in(key_of[9], part), 71), part),
        "list_weight": jnp.clip(jnp.exp(jax.random.uniform(own_keys[8], (LISTS,), jnp.float32, math.log(0.25), math.log(4.0))), 0.25, 4.0),
    }


def encode(block, w_in, w_out, gain):
    count, length, width = block.shape
    flat = block.reshape(count * length, width)
    hidden = jax.nn.gelu(jnp.dot(flat, w_in, preferred_element_type=jnp.float32), approximate=True).astype(jnp.bfloat16)
    mixed = flat.astype(jnp.float32) + jnp.dot(hidden, w_out, preferred_element_type=jnp.float32)
    centre = mixed - lax.optimization_barrier(jnp.mean(mixed, axis=-1, keepdims=True))
    spread = lax.optimization_barrier(jnp.mean(centre * centre, axis=-1, keepdims=True))
    normed = centre * lax.rsqrt(spread + 1e-05) * gain
    averaged = lax.optimization_barrier(jnp.mean(normed.reshape(count, length, width), axis=1))
    scale = lax.rsqrt(lax.optimization_barrier(jnp.mean(averaged * averaged, axis=-1, keepdims=True)) + 1e-06)
    return (averaged * scale).astype(jnp.bfloat16)

def code_table(codes, values, weight, n_codes):
    rows, width = values.shape
    parts = codes.shape[1]
    sub_width = width // parts
    block = math.gcd(rows, 128)
    turns = rows // block

    def step(index, carry):
        sums, counts = carry
        start = index * block
        code_blk = lax.dynamic_slice_in_dim(codes, start, block, 0)
        value_blk = lax.dynamic_slice_in_dim(values, start, block, 0).reshape(block, parts, sub_width)
        weight_blk = lax.dynamic_slice_in_dim(weight, start, block, 0)
        onehot = (code_blk[:, :, None] == jnp.arange(n_codes, dtype=jnp.int32)[None, None, :]).astype(values.dtype) * weight_blk[:, None, None]
        sums = sums + jnp.einsum('rmc,rmk->cmk', onehot, value_blk, precision=lax.Precision.HIGHEST)
        counts = counts + lax.optimization_barrier(jnp.sum(onehot, axis=0)).T
        return (sums, counts)
    start_val = (jnp.zeros((n_codes, parts, sub_width), values.dtype), jnp.zeros((n_codes, parts), values.dtype))
    sums, counts = lax.fori_loop(0, turns, step, start_val)
    return (sums.reshape(n_codes, width), counts)

def reference(tokens, w_in, w_out, gain, centroids, list_slot, assign, codes, list_weight):
    blocks = tokens.reshape(PASSAGES // P_DEV, P_DEV, LEN, D)
    pooled = lax.map(lambda block: encode(block, w_in, w_out, gain), blocks).reshape(PASSAGES, D)
    slot = jnp.take(list_slot, assign).astype(jnp.int32)
    weight = jnp.take(list_weight, assign)
    cent_rows = jnp.take(centroids, slot, axis=0).astype(jnp.float32)
    residual = pooled.astype(jnp.float32) - cent_rows
    sums, counts = code_table(codes, residual, weight, CODES)
    shaped = sums.reshape(CODES, M, D // M) / jnp.maximum(counts, 1.0)[:, :, None]
    codewords = shaped.reshape(CODES, D)
    list_sums = jax.ops.segment_sum(pooled.astype(jnp.float32), slot, num_segments=LISTS)
    list_counts = jax.ops.segment_sum(jnp.ones((PASSAGES,), jnp.float32), slot, num_segments=LISTS)
    updated = centroids + (list_sums - list_counts[:, None] * centroids) / (list_counts[:, None] + 1.0)
    return (updated.astype(jnp.bfloat16), codewords)
```

```python
import functools

import jax
import jax.numpy as jnp
from jax import lax
from jax.experimental import pallas as pl
from jax.experimental.pallas import tpu as pltpu
from jax.sharding import PartitionSpec as P

CODES = 256
LANES = 128
SUB = 16
BF, F32, I32 = jnp.bfloat16, jnp.float32, jnp.int32
MESH = pl.DeviceIdType.MESH


def up(value, step):
    return (value + step - 1) // step * step


def gelu(x):
    inner = x * (0.7978845608028654 + 0.035677408136300125 * (x * x))
    return 0.5 * x * (1.0 + jnp.tanh(inner))


def main_kernel(
    cfg,
    slot_row_ref, slot_col_ref, weight_ref, codes_ref, gain_ref,
    tok_hbm, win_hbm, wout_hbm, cent_hbm,
    rows_out, ids_out, code_out,
    tok, win, wout, cent, pooled,
    ids_send, ids_got, cent_send, cent_got, row_send, row_got,
    table, table16, got1, send2, got2, send3, got3,
    load_sem, id_s, id_r, cent_s, cent_r, row_s, row_r, t_s, t_r,
):
    L, S, lo, hi, cap, capp, slots_dev, held, heldp = cfg
    D = L * S
    width = tok.shape[1]
    passages = tok.shape[0] // 8
    padded = slot_row_ref.shape[1]
    li, si = lax.axis_index("lists"), lax.axis_index("sub")
    me = li * S + si
    hi_i, lo_i = li // lo, lax.rem(li, lo)
    ff = win.shape[1]
    nchunk = 4
    fc = ff // nchunk

    def dev(index):
        return {"lists": index // S, "sub": lax.rem(index, S)}

    loads = [pltpu.make_async_copy(tok_hbm, tok, load_sem.at[0])]
    for c in range(nchunk):
        loads.append(pltpu.make_async_copy(
            win_hbm.at[:, pl.ds(c * fc, fc)], win.at[:, pl.ds(c * fc, fc)], load_sem.at[1 + 2 * c]))
        loads.append(pltpu.make_async_copy(
            wout_hbm.at[pl.ds(c * fc, fc), :], wout.at[pl.ds(c * fc, fc), :], load_sem.at[2 + 2 * c]))
    cent_load = pltpu.make_async_copy(cent_hbm, cent, load_sem.at[1 + 2 * nchunk])
    for one in loads:
        one.start()
    cent_load.start()

    barrier = pltpu.get_barrier_semaphore()

    def greet(j, carry):
        pl.semaphore_signal(barrier, inc=1, device_id=dev(lax.rem(me + j, D)), device_id_type=MESH)
        return carry

    lax.fori_loop(1, D, greet, 0)

    shift = slots_dev.bit_length() - 1
    slot_row, slot_col = slot_row_ref[...], slot_col_ref[...]
    tr = jnp.where(slot_row >= 0, lax.shift_right_logical(slot_row, shift), -1)
    tc = jnp.where(slot_col >= 0, lax.shift_right_logical(slot_col, shift), -1)
    i0 = lax.broadcasted_iota(I32, (padded, padded), 0)
    i1 = lax.broadcasted_iota(I32, (padded, padded), 1)
    same = tr == tc
    rank_row = jnp.sum(jnp.where(same & (i0 < i1), 1.0, 0.0), axis=0, keepdims=True).astype(I32)
    rank_col = jnp.sum(jnp.where(same & (i1 < i0), 1.0, 0.0), axis=1, keepdims=True).astype(I32)
    dest_row = jnp.where(tr >= 0, tr * capp + rank_row, -1)
    dest_col = jnp.where(tc >= 0, tc * capp + rank_col, -1)
    local_row = (slot_row - jnp.maximum(tr, 0) * slots_dev + 1).astype(F32)
    di = lax.broadcasted_iota(I32, (D * capp, padded), 0)
    spread = di == dest_row
    ids = jnp.sum(jnp.where(spread, local_row, 0.0), axis=1, keepdims=True).astype(I32) - 1
    ids_send[...] = jnp.broadcast_to(ids, (D * capp, LANES)).reshape(D, capp, LANES)
    ids_got[me] = ids_send[me]

    pl.semaphore_wait(barrier, D - 1)

    def exchange(send, got, ss, rs):
        def start(j, carry):
            to = lax.rem(me + j, D)
            pltpu.make_async_remote_copy(
                src_ref=send.at[to], dst_ref=got.at[me], send_sem=ss.at[j], recv_sem=rs.at[j],
                device_id=dev(to), device_id_type=MESH).start()
            return carry

        lax.fori_loop(1, D, start, 0)

        def finish_recv():
            def body(j, carry):
                frm = lax.rem(me + D - j, D)
                pltpu.make_async_remote_copy(
                    src_ref=send.at[frm], dst_ref=got.at[frm], send_sem=ss.at[j],
                    recv_sem=rs.at[j], device_id=dev(frm), device_id_type=MESH).wait_recv()
                return carry
            lax.fori_loop(1, D, body, 0)

        def finish_send():
            def body(j, carry):
                to = lax.rem(me + j, D)
                pltpu.make_async_remote_copy(
                    src_ref=send.at[to], dst_ref=got.at[me], send_sem=ss.at[j],
                    recv_sem=rs.at[j], device_id=dev(to), device_id_type=MESH).wait_send()
                return carry
            lax.fori_loop(1, D, body, 0)

        return finish_recv, finish_send

    id_recv, id_sent = exchange(ids_send, ids_got, id_s, id_r)

    nblk = 3 if passages % 48 == 0 else 1
    per = passages // nblk
    toks = per * 8

    def encode(b, wait):
        x = tok[pl.ds(b * toks, toks), :]
        acc = x.astype(F32)
        for c in range(nchunk):
            if wait:
                loads[1 + 2 * c].wait()
            h = gelu(jnp.dot(x, win[:, c * fc:(c + 1) * fc], preferred_element_type=F32)).astype(BF)
            if wait:
                loads[2 + 2 * c].wait()
            acc = acc + jnp.dot(h, wout[c * fc:(c + 1) * fc, :], preferred_element_type=F32)
        centre = acc - jnp.mean(acc, axis=-1, keepdims=True)
        var = jnp.mean(centre * centre, axis=-1, keepdims=True)
        normed = centre * lax.rsqrt(var + 1e-05)
        avg = jnp.mean(normed.reshape(per, 8, width), axis=1) * gain_ref[...]
        scale = lax.rsqrt(jnp.mean(avg * avg, axis=-1, keepdims=True) + 1e-06)
        pooled[pl.ds(b * per, per), :] = (avg * scale).astype(BF)

    pooled[...] = jnp.zeros_like(pooled)
    loads[0].wait()
    encode(0, True)

    id_recv()
    cent_load.wait()
    want = ids_got[...].reshape(D * capp, LANES)
    ids_out[...] = want.T[0:8, :]
    rb = 256

    def pick(i, carry):
        start = pl.multiple_of(i * rb, rb)
        mine = ids_got[pl.ds(i * (rb // capp), rb // capp)].reshape(rb, LANES)[:, 0:1]
        hit = jnp.where(lax.broadcasted_iota(I32, (rb, slots_dev), 1) == mine, 1.0, 0.0).astype(BF)
        out = jnp.dot(hit, cent[...], preferred_element_type=F32).astype(BF)
        cent_send[pl.ds(i * (rb // capp), rb // capp)] = out.reshape(rb // capp, capp, width)
        return carry

    lax.fori_loop(0, D * capp // rb, pick, 0)
    cent_got[me] = cent_send[me]
    cent_recv, cent_sent = exchange(cent_send, cent_got, cent_s, cent_r)

    for b in range(1, nblk):
        encode(b, False)

    put = jnp.where(spread, 1.0, 0.0).astype(BF)
    row_send[...] = jnp.dot(put, pooled[...], preferred_element_type=F32).astype(BF).reshape(D, capp, width)
    row_got[me] = row_send[me]

    cent_recv()
    get = jnp.where(
        lax.broadcasted_iota(I32, (padded, D * capp), 1) == dest_col, 1.0, 0.0).astype(BF)
    cent_rows = jnp.dot(get, cent_got[...].reshape(D * capp, width), preferred_element_type=F32)
    weight = weight_ref[...]
    resid = ((pooled[...].astype(F32) - cent_rows) * weight).astype(BF)
    w_hi = weight.astype(BF).astype(F32)
    w_lo = weight - w_hi

    nrow = S * lo * hi * heldp
    tb = 256
    lane = lax.broadcasted_iota(I32, (padded, LANES), 1)
    group = LANES // SUB
    ngroup = width // LANES
    logical = {"hp": heldp.bit_length() - 1}

    def build(i, carry):
        t = lax.broadcasted_iota(I32, (tb, 1), 0) + i * tb
        k = jnp.bitwise_and(t, heldp - 1)
        rest = lax.shift_right_logical(t, logical["hp"])
        h = jnp.bitwise_and(rest, hi - 1)
        rest = lax.shift_right_logical(rest, hi.bit_length() - 1)
        l = jnp.bitwise_and(rest, lo - 1)
        s = lax.shift_right_logical(rest, lo.bit_length() - 1)
        code = jnp.where(k < held, ((h * lo + l) * S + s) * held + k, -2)
        counts = jnp.zeros((tb, LANES), F32)
        start = pl.multiple_of(i * tb, tb)
        for j in range(ngroup):
            lhs, rhs = [], []
            part = resid[:, j * LANES:(j + 1) * LANES]
            for mm in range(group):
                m = j * group + mm
                lhs.append(jnp.where(codes_ref[m:m + 1, :] == code, 1.0, 0.0).astype(BF))
                data = jnp.where(lane // SUB == mm, part.astype(F32), 0.0).astype(BF)
                cnt = jnp.where(lane == m, w_hi, jnp.where(lane == 64 + m, w_lo, 0.0)).astype(BF)
                rhs.append(jnp.concatenate([data, cnt], axis=1))
            out = jnp.dot(jnp.concatenate(lhs, axis=1), jnp.concatenate(rhs, axis=0),
                          preferred_element_type=F32)
            table[pl.ds(start, tb), j * LANES:(j + 1) * LANES] = out[:, :LANES]
            table16[pl.ds(start, tb), j * LANES:(j + 1) * LANES] = out[:, :LANES].astype(BF)
            counts = counts + out[:, LANES:]
        total = counts + pltpu.roll(counts, 64, 1)
        table[pl.ds(start, tb), width:] = total
        table16[pl.ds(start, tb), width:] = split(total)
        return carry

    def split(total):
        first = total.astype(BF)
        keep = lax.broadcasted_iota(I32, total.shape, 1) < 64
        return jnp.where(keep, first.astype(F32), total - first.astype(F32)).astype(BF)

    def joined(block):
        wide = block.astype(F32)
        tail = wide[:, width:]
        return jnp.concatenate([wide[:, :width], tail + pltpu.roll(tail, 64, 1)], axis=1)

    def narrow(block):
        return jnp.concatenate([block[:, :width].astype(BF), split(block[:, width:])], axis=1)

    lax.fori_loop(0, nrow // tb, build, 0)

    n1, n2 = lo * hi * heldp, hi * heldp

    def swap(src, dst, at, device):
        return pltpu.make_async_remote_copy(
            src_ref=src, dst_ref=dst, send_sem=t_s.at[at], recv_sem=t_r.at[at],
            device_id=device, device_id_type=MESH)

    other = 1 - si
    one = swap(table16.at[pl.ds(pl.multiple_of(other * n1, 16), n1)], got1, 0, {"lists": li, "sub": other})
    one.start()
    row_recv, row_sent = exchange(row_send, row_got, row_s, row_r)
    one.wait_recv()
    lo_o = 1 - lo_i
    mine1 = pl.multiple_of(si * n1, 16)
    away = pl.multiple_of(lo_o * n2, 16)
    near = pl.multiple_of(lo_i * n2, 16)
    send2[...] = narrow(table[pl.ds(mine1 + away, n2), :] + joined(got1[pl.ds(away, n2), :]))
    two = swap(send2, got2, 1, {"lists": hi_i * lo + lo_o, "sub": si})
    two.start()
    acc = table[pl.ds(mine1 + near, n2), :] + joined(got1[pl.ds(near, n2), :])
    two.wait_recv()
    acc = acc + joined(got2[...])
    table[0:n2, :] = acc
    send3[...] = narrow(acc).reshape(hi, heldp, width + LANES)

    def third(j, frm):
        return pltpu.make_async_remote_copy(
            src_ref=send3.at[lax.rem(hi_i + j, hi)], dst_ref=got3.at[frm],
            send_sem=t_s.at[2 + j], recv_sem=t_r.at[2 + j],
            device_id={"lists": lax.rem(hi_i + j, hi) * lo + lo_i, "sub": si}, device_id_type=MESH)

    def third_start(j, carry):
        third(j, hi_i).start()
        return carry

    lax.fori_loop(1, hi, third_start, 0)

    def third_recv(j, total):
        frm = lax.rem(hi_i + hi - j, hi)
        third(j, frm).wait_recv()
        return total + joined(got3[frm])

    total = lax.fori_loop(
        1, hi, third_recv, table[pl.ds(pl.multiple_of(hi_i * heldp, heldp), heldp), :])
    row = lax.broadcasted_iota(I32, (LANES, width), 0)
    col = lax.broadcasted_iota(I32, (LANES, width), 1)
    expand = jnp.where((row == col // SUB), 1.0, 0.0).astype(BF)
    inv = 1.0 / jnp.maximum(total[:, width:], 1.0)
    wide = jnp.zeros((heldp, width), F32)
    for _ in range(3):
        top = inv.astype(BF)
        wide = wide + jnp.dot(top, expand, preferred_element_type=F32)
        inv = inv - top.astype(F32)
    code_out[...] = (total[:, :width] * wide)[:held]

    row_recv()
    rows_out[...] = row_got[...].reshape(D * capp, width)

    id_sent()
    cent_sent()
    row_sent()
    one.wait_send()
    two.wait_send()

    def third_sent(j, carry):
        third(j, hi_i).wait_send()
        return carry

    lax.fori_loop(1, hi, third_sent, 0)


def update_kernel(ids_ref, rows_ref, cent_ref, out_ref):
    blk = cent_ref.shape[0]
    n = rows_ref.shape[0]
    base = pl.program_id(0) * blk
    slot = lax.broadcasted_iota(I32, (blk, n), 0) + base
    hit = jnp.where(slot == ids_ref[0:1, :], 1.0, 0.0)
    count = jnp.sum(hit, axis=1, keepdims=True)
    sums = jnp.dot(hit.astype(BF), rows_ref[...], preferred_element_type=F32)
    cent = cent_ref[...].astype(F32)
    out_ref[...] = (cent + (sums - count * cent) * (1.0 / (count + 1.0))).astype(BF)


def shards(tokens, w_in, w_out, gain, centroids, list_slot, assign, codes, list_weight):
    count, length, width = tokens.shape
    parts = codes.shape[1]
    slots_dev = centroids.shape[0]
    L, S = lax.axis_size("lists"), lax.axis_size("sub")
    D = L * S
    lo = 2
    hi = L // lo
    cap = max(2, (2 * count + D - 1) // D)
    capp = up(cap, 16)
    held = CODES // D
    heldp = up(held, 16)
    padded = up(count, LANES)
    ff = w_in.shape[1]
    wtab = width + LANES

    slot = jnp.pad(jnp.take(list_slot, assign), (0, padded - count), constant_values=-1)
    weight = jnp.pad(jnp.take(list_weight, assign), (0, padded - count))
    codes_t = jnp.pad(codes.T, ((0, 0), (0, padded - count)), constant_values=-1)

    cfg = (L, S, lo, hi, cap, capp, slots_dev, held, heldp)
    vm = pl.BlockSpec(memory_space=pltpu.VMEM)
    anyspace = pl.BlockSpec(memory_space=pl.ANY)
    n1, n2 = lo * hi * heldp, hi * heldp
    dma = pltpu.SemaphoreType.DMA
    rows, ids, codewords = pl.pallas_call(
        functools.partial(main_kernel, cfg),
        out_shape=(
            jax.ShapeDtypeStruct((D * capp, width), BF),
            jax.ShapeDtypeStruct((8, D * capp), I32),
            jax.ShapeDtypeStruct((held, width), F32),
        ),
        in_specs=[vm] * 5 + [anyspace] * 4,
        out_specs=(vm, vm, vm),
        scratch_shapes=[
            pltpu.VMEM((count * length, width), BF),
            pltpu.VMEM((width, ff), BF),
            pltpu.VMEM((ff, width), BF),
            pltpu.VMEM((slots_dev, width), BF),
            pltpu.VMEM((padded, width), BF),
            pltpu.VMEM((D, capp, LANES), I32),
            pltpu.VMEM((D, capp, LANES), I32),
            pltpu.VMEM((D, capp, width), BF),
            pltpu.VMEM((D, capp, width), BF),
            pltpu.VMEM((D, capp, width), BF),
            pltpu.VMEM((D, capp, width), BF),
            pltpu.VMEM((S * n1, wtab), F32),
            pltpu.VMEM((S * n1, wtab), BF),
            pltpu.VMEM((n1, wtab), BF),
            pltpu.VMEM((n2, wtab), BF),
            pltpu.VMEM((n2, wtab), BF),
            pltpu.VMEM((hi, heldp, wtab), BF),
            pltpu.VMEM((hi, heldp, wtab), BF),
            dma((16,)),
            dma((D,)), dma((D,)), dma((D,)), dma((D,)), dma((D,)), dma((D,)),
            dma((2 + hi,)), dma((2 + hi,)),
        ],
        compiler_params=pltpu.CompilerParams(
            collective_id=0, has_side_effects=True, vmem_limit_bytes=60 * 1024 * 1024),
        name="encode_route",
    )(
        slot.reshape(1, padded), slot.reshape(padded, 1), weight.reshape(padded, 1), codes_t,
        gain.reshape(1, width), tokens.reshape(count * length, width), w_in, w_out, centroids,
    )

    blk = min(512, slots_dev)
    updated = pl.pallas_call(
        update_kernel,
        grid=(slots_dev // blk,),
        out_shape=jax.ShapeDtypeStruct((slots_dev, width), BF),
        in_specs=[
            pl.BlockSpec((8, D * capp), lambda i: (0, 0)),
            pl.BlockSpec((D * capp, width), lambda i: (0, 0)),
            pl.BlockSpec((blk, width), lambda i: (i, 0)),
        ],
        out_specs=pl.BlockSpec((blk, width), lambda i: (i, 0)),
        compiler_params=pltpu.CompilerParams(vmem_limit_bytes=40 * 1024 * 1024),
        name="update_lists",
    )(ids, rows, centroids)
    return updated, codewords


def solution(mesh):
    return jax.shard_map(
        shards,
        mesh=mesh,
        in_specs=(
            P(("groups", "lists", "sub"), None, None),
            P(),
            P(),
            P(),
            P(("lists", "sub"), None),
            P("groups"),
            P(("groups", "lists", "sub")),
            P(("groups", "lists", "sub"), None),
            P("groups"),
        ),
        out_specs=(P(("groups", "lists", "sub"), None), P(("groups", "lists", "sub"), None)),
        check_vma=False,
    )
```

```python
import functools

import jax
import jax.numpy as jnp
from jax import lax
from jax.experimental import pallas as pl
from jax.experimental.pallas import tpu as pltpu
from jax.sharding import PartitionSpec as P

CODES = 256
LANES = 128
SUB = 16
BF, F32, I32 = jnp.bfloat16, jnp.float32, jnp.int32
MESH = pl.DeviceIdType.MESH


def up(value, step):
    return (value + step - 1) // step * step


def gelu(x):
    inner = x * (0.7978845608028654 + 0.035677408136300125 * (x * x))
    return 0.5 * x * (1.0 + jnp.tanh(inner))


def main_kernel(
    cfg,
    assign_ref, codes_in, gain_ref, slot_hbm, weight_hbm,
    tok_hbm, win_hbm, wout_hbm, cent_hbm,
    rows_out, ids_out, code_out,
    slot_tab, weight_tab, slot_hit, weight_hit, codes_pad, codes_ref,
    tok, win, wout, cent, pooled,
    ids_send, ids_got, cent_send, cent_got, row_send, row_got,
    table, acc3, got1, send2, got2, send3, got3,
    load_sem, id_s, id_r, cent_s, cent_r, row_s, row_r, t_s, t_r,
):
    L, S, lo, hi, cap, capp, slots_dev, held, heldp = cfg
    D = L * S
    width = tok.shape[1]
    passages = tok.shape[0] // 8
    padded = slot_hit.shape[0]
    li, si = lax.axis_index("lists"), lax.axis_index("sub")
    me = li * S + si
    hi_i, lo_i = li // lo, lax.rem(li, lo)
    ff = win.shape[1]
    nchunk = 4
    fc = ff // nchunk

    def dev(index):
        return {"lists": index // S, "sub": lax.rem(index, S)}

    loads = [pltpu.make_async_copy(tok_hbm, tok, load_sem.at[0])]
    for c in range(nchunk):
        loads.append(pltpu.make_async_copy(
            win_hbm.at[:, pl.ds(c * fc, fc)], win.at[:, pl.ds(c * fc, fc)], load_sem.at[1 + 2 * c]))
        loads.append(pltpu.make_async_copy(
            wout_hbm.at[pl.ds(c * fc, fc), :], wout.at[pl.ds(c * fc, fc), :], load_sem.at[2 + 2 * c]))
    cent_load = pltpu.make_async_copy(cent_hbm, cent, load_sem.at[1 + 2 * nchunk])
    slot_load = pltpu.make_async_copy(slot_hbm, slot_tab, load_sem.at[2 + 2 * nchunk])
    weight_load = pltpu.make_async_copy(weight_hbm, weight_tab, load_sem.at[3 + 2 * nchunk])
    slot_load.start()
    weight_load.start()
    cent_load.start()
    for one in loads:
        one.start()

    barrier = pltpu.get_barrier_semaphore()

    def greet(j, carry):
        pl.semaphore_signal(barrier, inc=1, device_id=dev(lax.rem(me + j, D)), device_id_type=MESH)
        return carry

    lax.fori_loop(1, D, greet, 0)

    shift = slots_dev.bit_length() - 1
    slot_hit[...] = jnp.zeros_like(slot_hit)
    weight_hit[...] = jnp.zeros_like(weight_hit)
    lane1 = lax.broadcasted_iota(I32, (1, LANES), 1)
    slot_load.wait()
    weight_load.wait()

    def look(p, carry):
        a = assign_ref[p]
        row = lax.shift_right_logical(a, 7)
        at = lane1 == jnp.bitwise_and(a, LANES - 1)
        slot_hit[pl.ds(p, 1), :] = jnp.where(at, slot_tab[pl.ds(row, 1), :].astype(F32), 0.0)
        weight_hit[pl.ds(p, 1), :] = jnp.where(at, weight_tab[pl.ds(row, 1), :], 0.0)
        return carry

    lax.fori_loop(0, passages, look, 0, unroll=8)
    below = lax.broadcasted_iota(I32, (padded, 1), 0) < passages
    slot_f = jnp.where(below, jnp.sum(slot_hit[...], axis=1, keepdims=True), -1.0)
    slot_col = slot_f.astype(I32)
    i0 = lax.broadcasted_iota(I32, (padded, padded), 0)
    i1 = lax.broadcasted_iota(I32, (padded, padded), 1)
    slot_row = jnp.sum(jnp.where(i0 == i1, slot_f, 0.0), axis=0, keepdims=True).astype(I32)
    tr = jnp.where(slot_row >= 0, lax.shift_right_logical(slot_row, shift), -1)
    tc = jnp.where(slot_col >= 0, lax.shift_right_logical(slot_col, shift), -1)
    same = tr == tc
    rank_row = jnp.sum(jnp.where(same & (i0 < i1), 1.0, 0.0), axis=0, keepdims=True).astype(I32)
    rank_col = jnp.sum(jnp.where(same & (i1 < i0), 1.0, 0.0), axis=1, keepdims=True).astype(I32)
    dest_row = jnp.where(tr >= 0, tr * capp + rank_row, -1)
    dest_col = jnp.where(tc >= 0, tc * capp + rank_col, -1)
    local_row = (slot_row - jnp.maximum(tr, 0) * slots_dev + 1).astype(F32)
    di = lax.broadcasted_iota(I32, (D * capp, padded), 0)
    spread = di == dest_row
    ids = jnp.sum(jnp.where(spread, local_row, 0.0), axis=1, keepdims=True).astype(I32) - 1
    ids_send[...] = jnp.broadcast_to(ids, (D * capp, LANES)).reshape(D, capp, LANES)
    ids_got[me] = ids_send[me]

    pl.semaphore_wait(barrier, D - 1)

    def exchange(send, got, ss, rs):
        def start(j, carry):
            to = lax.rem(me + j, D)
            pltpu.make_async_remote_copy(
                src_ref=send.at[to], dst_ref=got.at[me], send_sem=ss.at[j], recv_sem=rs.at[j],
                device_id=dev(to), device_id_type=MESH).start()
            return carry

        lax.fori_loop(1, D, start, 0)

        def finish_recv():
            def body(j, carry):
                frm = lax.rem(me + D - j, D)
                pltpu.make_async_remote_copy(
                    src_ref=send.at[frm], dst_ref=got.at[frm], send_sem=ss.at[j],
                    recv_sem=rs.at[j], device_id=dev(frm), device_id_type=MESH).wait_recv()
                return carry
            lax.fori_loop(1, D, body, 0)

        def finish_send():
            def body(j, carry):
                to = lax.rem(me + j, D)
                pltpu.make_async_remote_copy(
                    src_ref=send.at[to], dst_ref=got.at[me], send_sem=ss.at[j],
                    recv_sem=rs.at[j], device_id=dev(to), device_id_type=MESH).wait_send()
                return carry
            lax.fori_loop(1, D, body, 0)

        return finish_recv, finish_send

    id_recv, id_sent = exchange(ids_send, ids_got, id_s, id_r)

    nblk = 3 if passages % 48 == 0 else 1
    per = passages // nblk
    toks = per * 8

    def encode(b, wait):
        x = tok[pl.ds(b * toks, toks), :]
        acc = x.astype(F32)
        for c in range(nchunk):
            if wait:
                loads[1 + 2 * c].wait()
            h = gelu(jnp.dot(x, win[:, c * fc:(c + 1) * fc], preferred_element_type=F32)).astype(BF)
            if wait:
                loads[2 + 2 * c].wait()
            acc = acc + jnp.dot(h, wout[c * fc:(c + 1) * fc, :], preferred_element_type=F32)
        centre = acc - jnp.mean(acc, axis=-1, keepdims=True)
        var = jnp.mean(centre * centre, axis=-1, keepdims=True)
        normed = centre * lax.rsqrt(var + 1e-05)
        avg = jnp.mean(normed.reshape(per, 8, width), axis=1) * gain_ref[...]
        scale = lax.rsqrt(jnp.mean(avg * avg, axis=-1, keepdims=True) + 1e-06)
        pooled[pl.ds(b * per, per), :] = (avg * scale).astype(BF)

    id_recv()
    cent_load.wait()
    want = ids_got[...].reshape(D * capp, LANES)
    ids_out[...] = want.T[0:8, :]
    rb = 256

    def pick(i, carry):
        start = pl.multiple_of(i * rb, rb)
        mine = ids_got[pl.ds(i * (rb // capp), rb // capp)].reshape(rb, LANES)[:, 0:1]
        hit = jnp.where(lax.broadcasted_iota(I32, (rb, slots_dev), 1) == mine, 1.0, 0.0).astype(BF)
        out = jnp.dot(hit, cent[...], preferred_element_type=F32).astype(BF)
        cent_send[pl.ds(i * (rb // capp), rb // capp)] = out.reshape(rb // capp, capp, width)
        return carry

    lax.fori_loop(0, D * capp // rb, pick, 0)
    cent_got[me] = cent_send[me]
    cent_recv, cent_sent = exchange(cent_send, cent_got, cent_s, cent_r)

    codes_pad[...] = jnp.full(codes_pad.shape, -1.0, F32)
    codes_pad[0:passages, 0:codes_in.shape[1]] = codes_in[...].astype(F32)
    codes_ref[...] = codes_pad[...].T

    pooled[...] = jnp.zeros_like(pooled)
    loads[0].wait()
    for b in range(nblk):
        encode(b, b == 0)

    put = jnp.where(spread, 1.0, 0.0).astype(BF)
    row_send[...] = jnp.dot(put, pooled[...], preferred_element_type=F32).astype(BF).reshape(D, capp, width)
    row_got[me] = row_send[me]
    row_recv, row_sent = exchange(row_send, row_got, row_s, row_r)

    cent_recv()
    get = jnp.where(
        lax.broadcasted_iota(I32, (padded, D * capp), 1) == dest_col, 1.0, 0.0).astype(BF)
    cent_rows = jnp.dot(get, cent_got[...].reshape(D * capp, width), preferred_element_type=F32)
    weight = jnp.sum(weight_hit[...], axis=1, keepdims=True)
    resid = (pooled[...].astype(F32) - cent_rows) * weight
    r_hi = resid.astype(BF).astype(F32)
    r_lo = resid - r_hi
    w_hi = weight.astype(BF).astype(F32)
    w_lo = weight - w_hi

    nrow = S * lo * hi * heldp
    tb = 256
    lane = lax.broadcasted_iota(I32, (padded, LANES), 1)
    group = LANES // SUB
    ngroup = width // LANES
    logical = {"hp": heldp.bit_length() - 1}

    def build(i, carry):
        t = lax.broadcasted_iota(I32, (tb, 1), 0) + i * tb
        k = jnp.bitwise_and(t, heldp - 1)
        rest = lax.shift_right_logical(t, logical["hp"])
        h = jnp.bitwise_and(rest, hi - 1)
        rest = lax.shift_right_logical(rest, hi.bit_length() - 1)
        l = jnp.bitwise_and(rest, lo - 1)
        s = lax.shift_right_logical(rest, lo.bit_length() - 1)
        code = jnp.where(k < held, ((h * lo + l) * S + s) * held + k, -2).astype(F32)
        counts = jnp.zeros((tb, LANES), F32)
        start = pl.multiple_of(i * tb, tb)
        for j in range(ngroup):
            lhs, rhs = [], []
            part_hi = r_hi[:, j * LANES:(j + 1) * LANES]
            part_lo = r_lo[:, j * LANES:(j + 1) * LANES]
            for mm in range(group):
                m = j * group + mm
                lhs.append(jnp.where(codes_ref[m:m + 1, :] == code, 1.0, 0.0).astype(BF))
                own = lane // SUB == mm
                data = jnp.where(own, part_hi, 0.0).astype(BF)
                rest_data = jnp.where(own, part_lo, 0.0).astype(BF)
                cnt = jnp.where(lane == m, w_hi, jnp.where(lane == 64 + m, w_lo, 0.0)).astype(BF)
                rhs.append(jnp.concatenate([data, rest_data, cnt], axis=1))
            out = jnp.dot(jnp.concatenate(lhs, axis=1), jnp.concatenate(rhs, axis=0),
                          preferred_element_type=F32)
            table[pl.ds(start, tb), j * LANES:(j + 1) * LANES] = (
                out[:, :LANES] + out[:, LANES:2 * LANES])
            counts = counts + out[:, 2 * LANES:]
        total = counts + pltpu.roll(counts, 64, 1)
        table[pl.ds(start, tb), width:] = total
        return carry

    def split(total):
        first = total.astype(BF)
        keep = lax.broadcasted_iota(I32, total.shape, 1) < 64
        return jnp.where(keep, first.astype(F32), total - first.astype(F32)).astype(BF)

    def joined(block):
        wide = block.astype(F32)
        tail = wide[:, width:]
        return jnp.concatenate([wide[:, :width], tail + pltpu.roll(tail, 64, 1)], axis=1)

    def narrow(block):
        return jnp.concatenate([block[:, :width].astype(BF), split(block[:, width:])], axis=1)

    lax.fori_loop(0, nrow // tb, build, 0)

    n1, n2 = lo * hi * heldp, hi * heldp

    def swap(src, dst, at, device):
        return pltpu.make_async_remote_copy(
            src_ref=src, dst_ref=dst, send_sem=t_s.at[at], recv_sem=t_r.at[at],
            device_id=device, device_id_type=MESH)

    other = 1 - si
    one = swap(table.at[pl.ds(pl.multiple_of(other * n1, 16), n1)], got1, 0, {"lists": li, "sub": other})
    one.start()
    one.wait_recv()
    lo_o = 1 - lo_i
    mine1 = pl.multiple_of(si * n1, 16)
    away = pl.multiple_of(lo_o * n2, 16)
    near = pl.multiple_of(lo_i * n2, 16)
    send2[...] = narrow(table[pl.ds(mine1 + away, n2), :] + got1[pl.ds(away, n2), :])
    two = swap(send2, got2, 1, {"lists": hi_i * lo + lo_o, "sub": si})
    two.start()
    acc = table[pl.ds(mine1 + near, n2), :] + got1[pl.ds(near, n2), :]
    two.wait_recv()
    acc = acc + joined(got2[...])
    acc3[...] = acc.reshape(hi, heldp, width + LANES)
    send3[...] = narrow(acc).reshape(hi, heldp, width + LANES)

    def third(j, frm):
        return pltpu.make_async_remote_copy(
            src_ref=send3.at[lax.rem(hi_i + j, hi)], dst_ref=got3.at[frm],
            send_sem=t_s.at[2 + j], recv_sem=t_r.at[2 + j],
            device_id={"lists": lax.rem(hi_i + j, hi) * lo + lo_i, "sub": si}, device_id_type=MESH)

    def third_start(j, carry):
        third(j, hi_i).start()
        return carry

    lax.fori_loop(1, hi, third_start, 0)

    def third_recv(j, total):
        frm = lax.rem(hi_i + hi - j, hi)
        third(j, frm).wait_recv()
        return total + joined(got3[frm])

    total = lax.fori_loop(
        1, hi, third_recv, acc3[hi_i])
    row = lax.broadcasted_iota(I32, (LANES, width), 0)
    col = lax.broadcasted_iota(I32, (LANES, width), 1)
    expand = jnp.where((row == col // SUB), 1.0, 0.0).astype(BF)
    inv = 1.0 / jnp.maximum(total[:, width:], 1.0)
    wide = jnp.zeros((heldp, width), F32)
    for _ in range(3):
        top = inv.astype(BF)
        wide = wide + jnp.dot(top, expand, preferred_element_type=F32)
        inv = inv - top.astype(F32)
    code_out[...] = (total[:, :width] * wide)[:held]

    row_recv()
    rows_out[...] = row_got[...].reshape(D * capp, width)

    id_sent()
    cent_sent()
    row_sent()
    one.wait_send()
    two.wait_send()

    def third_sent(j, carry):
        third(j, hi_i).wait_send()
        return carry

    lax.fori_loop(1, hi, third_sent, 0)


def update_kernel(ids_ref, rows_ref, cent_ref, out_ref):
    blk = cent_ref.shape[0]
    n = rows_ref.shape[0]
    base = pl.program_id(0) * blk
    slot = lax.broadcasted_iota(I32, (blk, n), 0) + base
    hit = jnp.where(slot == ids_ref[0:1, :], 1.0, 0.0)
    count = jnp.sum(hit, axis=1, keepdims=True)
    sums = jnp.dot(hit.astype(BF), rows_ref[...], preferred_element_type=F32)
    cent = cent_ref[...].astype(F32)
    out_ref[...] = (cent + (sums - count * cent) * (1.0 / (count + 1.0))).astype(BF)


def shards(tokens, w_in, w_out, gain, centroids, list_slot, assign, codes, list_weight):
    count, length, width = tokens.shape
    slots_dev = centroids.shape[0]
    L, S = lax.axis_size("lists"), lax.axis_size("sub")
    D = L * S
    lo = 2
    hi = L // lo
    cap = max(2, (2 * count + D - 1) // D)
    capp = up(cap, 16)
    held = CODES // D
    heldp = up(held, 16)
    padded = up(count, LANES)
    ff = w_in.shape[1]
    wtab = width + LANES

    cfg = (L, S, lo, hi, cap, capp, slots_dev, held, heldp)
    vm = pl.BlockSpec(memory_space=pltpu.VMEM)
    anyspace = pl.BlockSpec(memory_space=pl.ANY)
    n1, n2 = lo * hi * heldp, hi * heldp
    dma = pltpu.SemaphoreType.DMA
    rows, ids, codewords = pl.pallas_call(
        functools.partial(main_kernel, cfg),
        out_shape=(
            jax.ShapeDtypeStruct((D * capp, width), BF),
            jax.ShapeDtypeStruct((8, D * capp), I32),
            jax.ShapeDtypeStruct((held, width), F32),
        ),
        in_specs=[pl.BlockSpec(memory_space=pltpu.SMEM)] + [vm] * 2 + [anyspace] * 6,
        out_specs=(vm, vm, vm),
        scratch_shapes=[
            pltpu.VMEM((list_slot.shape[0] // LANES, LANES), I32),
            pltpu.VMEM((list_slot.shape[0] // LANES, LANES), F32),
            pltpu.VMEM((padded, LANES), F32),
            pltpu.VMEM((padded, LANES), F32),
            pltpu.VMEM((padded, LANES), F32),
            pltpu.VMEM((LANES, padded), F32),
            pltpu.VMEM((count * length, width), BF),
            pltpu.VMEM((width, ff), BF),
            pltpu.VMEM((ff, width), BF),
            pltpu.VMEM((slots_dev, width), BF),
            pltpu.VMEM((padded, width), BF),
            pltpu.VMEM((D, capp, LANES), I32),
            pltpu.VMEM((D, capp, LANES), I32),
            pltpu.VMEM((D, capp, width), BF),
            pltpu.VMEM((D, capp, width), BF),
            pltpu.VMEM((D, capp, width), BF),
            pltpu.VMEM((D, capp, width), BF),
            pltpu.VMEM((S * n1, wtab), F32),
            pltpu.VMEM((hi, heldp, wtab), F32),
            pltpu.VMEM((n1, wtab), F32),
            pltpu.VMEM((n2, wtab), BF),
            pltpu.VMEM((n2, wtab), BF),
            pltpu.VMEM((hi, heldp, wtab), BF),
            pltpu.VMEM((hi, heldp, wtab), BF),
            dma((16,)),
            dma((D,)), dma((D,)), dma((D,)), dma((D,)), dma((D,)), dma((D,)),
            dma((2 + hi,)), dma((2 + hi,)),
        ],
        compiler_params=pltpu.CompilerParams(
            collective_id=0, has_side_effects=True, vmem_limit_bytes=60 * 1024 * 1024),
        name="encode_route",
    )(
        assign, codes, gain.reshape(1, width),
        list_slot.reshape(-1, LANES), list_weight.reshape(-1, LANES), tokens.reshape(count * length, width), w_in, w_out, centroids,
    )

    blk = min(512, slots_dev)
    updated = pl.pallas_call(
        update_kernel,
        grid=(slots_dev // blk,),
        out_shape=jax.ShapeDtypeStruct((slots_dev, width), BF),
        in_specs=[
            pl.BlockSpec((8, D * capp), lambda i: (0, 0)),
            pl.BlockSpec((D * capp, width), lambda i: (0, 0)),
            pl.BlockSpec((blk, width), lambda i: (i, 0)),
        ],
        out_specs=pl.BlockSpec((blk, width), lambda i: (i, 0)),
        compiler_params=pltpu.CompilerParams(vmem_limit_bytes=62 * 1024 * 1024),
        name="update_lists",
    )(ids, rows, centroids)
    return updated, codewords


def solution(mesh):
    return jax.shard_map(
        shards,
        mesh=mesh,
        in_specs=(
            P(("groups", "lists", "sub"), None, None),
            P(),
            P(),
            P(),
            P(("lists", "sub"), None),
            P("groups"),
            P(("groups", "lists", "sub")),
            P(("groups", "lists", "sub"), None),
            P("groups"),
        ),
        out_specs=(P(("groups", "lists", "sub"), None), P(("groups", "lists", "sub"), None)),
        check_vma=False,
    )
```

```python
import functools

import jax
import jax.numpy as jnp
from jax import lax
from jax.experimental import pallas as pl
from jax.experimental.pallas import tpu as pltpu
from jax.sharding import PartitionSpec as P

CODES = 256
LANES = 128
SUB = 16
BF, F32, I32 = jnp.bfloat16, jnp.float32, jnp.int32
MESH = pl.DeviceIdType.MESH


def up(value, step):
    return (value + step - 1) // step * step


def gelu(x):
    inner = x * (0.7978845608028654 + 0.035677408136300125 * (x * x))
    return 0.5 * x * (1.0 + jnp.tanh(inner))


def main_kernel(
    cfg,
    assign_ref, codes_in, gain_ref, slot_hbm, weight_hbm,
    tok_hbm, win_hbm, wout_hbm, cent_hbm,
    rows_out, ids_out, code_out,
    slot_tab, weight_tab, slot_hit, weight_hit, codes_pad, codes_ref,
    tok, win, wout, cent, pooled,
    ids_send, ids_got, cent_send, cent_got, row_send, row_got,
    table, acc3, got1, send2, got2, send3, got3,
    load_sem, id_s, id_r, cent_s, cent_r, row_s, row_r, t_s, t_r,
):
    L, S, lo, hi, cap, capp, cuts, slots_dev, held, heldp = cfg
    D = L * S
    width = tok.shape[1]
    wq, qc = width // cuts, cuts * cap
    passages = tok.shape[0] // 8
    padded = slot_hit.shape[0]
    li, si = lax.axis_index("lists"), lax.axis_index("sub")
    me = li * S + si
    hi_i, lo_i = li // lo, lax.rem(li, lo)
    ff = win.shape[1]
    nchunk = 4
    fc = ff // nchunk

    def dev(index):
        return {"lists": index // S, "sub": lax.rem(index, S)}

    loads = [pltpu.make_async_copy(tok_hbm, tok, load_sem.at[0])]
    for c in range(nchunk):
        loads.append(pltpu.make_async_copy(
            win_hbm.at[:, pl.ds(c * fc, fc)], win.at[:, pl.ds(c * fc, fc)], load_sem.at[1 + 2 * c]))
        loads.append(pltpu.make_async_copy(
            wout_hbm.at[pl.ds(c * fc, fc), :], wout.at[pl.ds(c * fc, fc), :], load_sem.at[2 + 2 * c]))
    cent_load = pltpu.make_async_copy(cent_hbm, cent, load_sem.at[1 + 2 * nchunk])
    slot_load = pltpu.make_async_copy(slot_hbm, slot_tab, load_sem.at[2 + 2 * nchunk])
    weight_load = pltpu.make_async_copy(weight_hbm, weight_tab, load_sem.at[3 + 2 * nchunk])
    slot_load.start()
    weight_load.start()
    cent_load.start()
    for one in loads:
        one.start()

    barrier = pltpu.get_barrier_semaphore()

    def greet(j, carry):
        pl.semaphore_signal(barrier, inc=1, device_id=dev(lax.rem(me + j, D)), device_id_type=MESH)
        return carry

    lax.fori_loop(1, D, greet, 0)

    shift = slots_dev.bit_length() - 1
    slot_hit[...] = jnp.zeros_like(slot_hit)
    weight_hit[...] = jnp.zeros_like(weight_hit)
    lane1 = lax.broadcasted_iota(I32, (1, LANES), 1)
    slot_load.wait()
    weight_load.wait()

    def look(p, carry):
        a = assign_ref[p]
        row = lax.shift_right_logical(a, 7)
        at = lane1 == jnp.bitwise_and(a, LANES - 1)
        slot_hit[pl.ds(p, 1), :] = jnp.where(at, slot_tab[pl.ds(row, 1), :].astype(F32), 0.0)
        weight_hit[pl.ds(p, 1), :] = jnp.where(at, weight_tab[pl.ds(row, 1), :], 0.0)
        return carry

    lax.fori_loop(0, passages, look, 0, unroll=8)
    below = lax.broadcasted_iota(I32, (padded, 1), 0) < passages
    slot_f = jnp.where(below, jnp.sum(slot_hit[...], axis=1, keepdims=True), -1.0)
    slot_col = slot_f.astype(I32)
    i0 = lax.broadcasted_iota(I32, (padded, padded), 0)
    i1 = lax.broadcasted_iota(I32, (padded, padded), 1)
    slot_row = jnp.sum(jnp.where(i0 == i1, slot_f, 0.0), axis=0, keepdims=True).astype(I32)
    tr = jnp.where(slot_row >= 0, lax.shift_right_logical(slot_row, shift), -1)
    tc = jnp.where(slot_col >= 0, lax.shift_right_logical(slot_col, shift), -1)
    same = tr == tc
    rank_row = jnp.sum(jnp.where(same & (i0 < i1), 1.0, 0.0), axis=0, keepdims=True).astype(I32)
    rank_col = jnp.sum(jnp.where(same & (i1 < i0), 1.0, 0.0), axis=1, keepdims=True).astype(I32)
    dest_row = jnp.where(tr >= 0, tr * capp + rank_row, -1)
    packed_row = jnp.where(tr >= 0, tr * qc + rank_row, -(1 << 20))
    packed_col = jnp.where(tc >= 0, tc * qc + rank_col, -(1 << 20))
    local_row = (slot_row - jnp.maximum(tr, 0) * slots_dev + 1).astype(F32)
    di = lax.broadcasted_iota(I32, (D * capp, padded), 0)
    spread = di == dest_row
    ids = jnp.sum(jnp.where(spread, local_row, 0.0), axis=1, keepdims=True).astype(I32) - 1
    ids_send[...] = jnp.broadcast_to(ids, (D * capp, LANES)).reshape(D, capp, LANES)
    ids_got[me] = ids_send[me]

    pl.semaphore_wait(barrier, D - 1)

    def exchange(send, got, ss, rs):
        def start(j, carry):
            to = lax.rem(me + j, D)
            pltpu.make_async_remote_copy(
                src_ref=send.at[to], dst_ref=got.at[me], send_sem=ss.at[j], recv_sem=rs.at[j],
                device_id=dev(to), device_id_type=MESH).start()
            return carry

        lax.fori_loop(1, D, start, 0)

        def finish_recv():
            def body(j, carry):
                frm = lax.rem(me + D - j, D)
                pltpu.make_async_remote_copy(
                    src_ref=send.at[frm], dst_ref=got.at[frm], send_sem=ss.at[j],
                    recv_sem=rs.at[j], device_id=dev(frm), device_id_type=MESH).wait_recv()
                return carry
            lax.fori_loop(1, D, body, 0)

        def finish_send():
            def body(j, carry):
                to = lax.rem(me + j, D)
                pltpu.make_async_remote_copy(
                    src_ref=send.at[to], dst_ref=got.at[me], send_sem=ss.at[j],
                    recv_sem=rs.at[j], device_id=dev(to), device_id_type=MESH).wait_send()
                return carry
            lax.fori_loop(1, D, body, 0)

        return finish_recv, finish_send

    id_recv, id_sent = exchange(ids_send, ids_got, id_s, id_r)

    nblk = 3 if passages % 48 == 0 else 1
    per = passages // nblk
    toks = per * 8

    def encode(b, wait):
        x = tok[pl.ds(b * toks, toks), :]
        acc = x.astype(F32)
        for c in range(nchunk):
            if wait:
                loads[1 + 2 * c].wait()
            h = gelu(jnp.dot(x, win[:, c * fc:(c + 1) * fc], preferred_element_type=F32)).astype(BF)
            if wait:
                loads[2 + 2 * c].wait()
            acc = acc + jnp.dot(h, wout[c * fc:(c + 1) * fc, :], preferred_element_type=F32)
        centre = acc - jnp.mean(acc, axis=-1, keepdims=True)
        var = jnp.mean(centre * centre, axis=-1, keepdims=True)
        normed = centre * lax.rsqrt(var + 1e-05)
        avg = jnp.mean(normed.reshape(per, 8, width), axis=1) * gain_ref[...]
        scale = lax.rsqrt(jnp.mean(avg * avg, axis=-1, keepdims=True) + 1e-06)
        pooled[pl.ds(b * per, per), :] = (avg * scale).astype(BF)

    id_recv()
    cent_load.wait()
    want = ids_got[...].reshape(D * capp, LANES)
    ids_out[...] = want.T[0:8, :]
    rb = 256
    rblk = rb // capp
    cbits = capp.bit_length() - 1

    def stacked(rows):
        return jnp.concatenate([rows[:, q * wq:(q + 1) * wq] for q in range(cuts)], axis=0)

    def place(index, q):
        r = jnp.bitwise_and(index, capp - 1)
        d = lax.shift_right_logical(index, cbits)
        return jnp.where(r < cap, d * qc + q * cap + r, -1)

    index_row = lax.broadcasted_iota(I32, (1, rb), 1)
    index_col = lax.broadcasted_iota(I32, (rb, 1), 0)
    pack = jnp.concatenate([place(index_row, q) for q in range(cuts)], axis=1)
    pack = jnp.where(lax.broadcasted_iota(I32, (rblk * qc, cuts * rb), 0) == pack, 1.0, 0.0).astype(BF)

    def pick(i, carry):
        mine = ids_got[pl.ds(i * rblk, rblk)].reshape(rb, LANES)[:, 0:1]
        hit = jnp.where(lax.broadcasted_iota(I32, (rb, slots_dev), 1) == mine, 1.0, 0.0).astype(BF)
        out = jnp.dot(hit, cent[...], preferred_element_type=F32).astype(BF)
        out = jnp.dot(pack, stacked(out), preferred_element_type=F32).astype(BF)
        cent_send[pl.ds(i * rblk, rblk)] = out.reshape(rblk, qc, wq)
        return carry

    lax.fori_loop(0, D * capp // rb, pick, 0)
    cent_got[me] = cent_send[me]
    cent_recv, cent_sent = exchange(cent_send, cent_got, cent_s, cent_r)

    codes_pad[...] = jnp.full(codes_pad.shape, -1.0, F32)
    codes_pad[0:passages, 0:codes_in.shape[1]] = codes_in[...].astype(F32)
    codes_ref[...] = codes_pad[...].T

    pooled[...] = jnp.zeros_like(pooled)
    loads[0].wait()
    for b in range(nblk):
        encode(b, b == 0)

    put = jnp.concatenate([packed_row + q * cap for q in range(cuts)], axis=1)
    put = jnp.where(
        lax.broadcasted_iota(I32, (D * qc, cuts * padded), 0) == put, 1.0, 0.0).astype(BF)
    row_send[...] = jnp.dot(
        put, stacked(pooled[...]), preferred_element_type=F32).astype(BF).reshape(D, qc, wq)
    row_got[me] = row_send[me]
    row_recv, row_sent = exchange(row_send, row_got, row_s, row_r)

    cent_recv()
    got_flat = cent_got[...].reshape(D * qc, wq)
    get_at = lax.broadcasted_iota(I32, (padded, D * qc), 1)
    cent_rows = jnp.concatenate([
        jnp.dot(jnp.where(get_at == packed_col + q * cap, 1.0, 0.0).astype(BF), got_flat,
                preferred_element_type=F32) for q in range(cuts)], axis=1)
    weight = jnp.sum(weight_hit[...], axis=1, keepdims=True)
    resid = (pooled[...].astype(F32) - cent_rows) * weight
    r_hi = resid.astype(BF).astype(F32)
    r_lo = resid - r_hi
    w_hi = weight.astype(BF).astype(F32)
    w_lo = weight - w_hi

    nrow = S * lo * hi * heldp
    tb = 256
    lane = lax.broadcasted_iota(I32, (padded, LANES), 1)
    group = LANES // SUB
    ngroup = width // LANES
    logical = {"hp": heldp.bit_length() - 1}

    def build(i, carry):
        t = lax.broadcasted_iota(I32, (tb, 1), 0) + i * tb
        k = jnp.bitwise_and(t, heldp - 1)
        rest = lax.shift_right_logical(t, logical["hp"])
        h = jnp.bitwise_and(rest, hi - 1)
        rest = lax.shift_right_logical(rest, hi.bit_length() - 1)
        l = jnp.bitwise_and(rest, lo - 1)
        s = lax.shift_right_logical(rest, lo.bit_length() - 1)
        code = jnp.where(k < held, ((h * lo + l) * S + s) * held + k, -2).astype(F32)
        counts = jnp.zeros((tb, LANES), F32)
        start = pl.multiple_of(i * tb, tb)
        for j in range(ngroup):
            lhs, rhs = [], []
            part_hi = r_hi[:, j * LANES:(j + 1) * LANES]
            part_lo = r_lo[:, j * LANES:(j + 1) * LANES]
            for mm in range(group):
                m = j * group + mm
                lhs.append(jnp.where(codes_ref[m:m + 1, :] == code, 1.0, 0.0).astype(BF))
                own = lane // SUB == mm
                data = jnp.where(own, part_hi, 0.0).astype(BF)
                rest_data = jnp.where(own, part_lo, 0.0).astype(BF)
                cnt = jnp.where(lane == m, w_hi, jnp.where(lane == 64 + m, w_lo, 0.0)).astype(BF)
                rhs.append(jnp.concatenate([data, rest_data, cnt], axis=1))
            out = jnp.dot(jnp.concatenate(lhs, axis=1), jnp.concatenate(rhs, axis=0),
                          preferred_element_type=F32)
            table[pl.ds(start, tb), j * LANES:(j + 1) * LANES] = (
                out[:, :LANES] + out[:, LANES:2 * LANES])
            counts = counts + out[:, 2 * LANES:]
        total = counts + pltpu.roll(counts, 64, 1)
        table[pl.ds(start, tb), width:] = total
        return carry

    def split(total):
        first = total.astype(BF)
        keep = lax.broadcasted_iota(I32, total.shape, 1) < 64
        return jnp.where(keep, first.astype(F32), total - first.astype(F32)).astype(BF)

    def joined(block):
        wide = block.astype(F32)
        tail = wide[:, width:]
        return jnp.concatenate([wide[:, :width], tail + pltpu.roll(tail, 64, 1)], axis=1)

    def narrow(block):
        return jnp.concatenate([block[:, :width].astype(BF), split(block[:, width:])], axis=1)

    lax.fori_loop(0, nrow // tb, build, 0)

    n1, n2 = lo * hi * heldp, hi * heldp

    def swap(src, dst, at, device):
        return pltpu.make_async_remote_copy(
            src_ref=src, dst_ref=dst, send_sem=t_s.at[at], recv_sem=t_r.at[at],
            device_id=device, device_id_type=MESH)

    other = 1 - si
    one = swap(table.at[pl.ds(pl.multiple_of(other * n1, 16), n1)], got1, 0, {"lists": li, "sub": other})
    one.start()
    one.wait_recv()
    lo_o = 1 - lo_i
    mine1 = pl.multiple_of(si * n1, 16)
    away = pl.multiple_of(lo_o * n2, 16)
    near = pl.multiple_of(lo_i * n2, 16)
    send2[...] = narrow(table[pl.ds(mine1 + away, n2), :] + got1[pl.ds(away, n2), :])
    two = swap(send2, got2, 1, {"lists": hi_i * lo + lo_o, "sub": si})
    two.start()
    acc = table[pl.ds(mine1 + near, n2), :] + got1[pl.ds(near, n2), :]
    two.wait_recv()
    acc = acc + joined(got2[...])
    acc3[...] = acc.reshape(hi, heldp, width + LANES)
    send3[...] = narrow(acc).reshape(hi, heldp, width + LANES)

    def third(j, frm):
        return pltpu.make_async_remote_copy(
            src_ref=send3.at[lax.rem(hi_i + j, hi)], dst_ref=got3.at[frm],
            send_sem=t_s.at[2 + j], recv_sem=t_r.at[2 + j],
            device_id={"lists": lax.rem(hi_i + j, hi) * lo + lo_i, "sub": si}, device_id_type=MESH)

    def third_start(j, carry):
        third(j, hi_i).start()
        return carry

    lax.fori_loop(1, hi, third_start, 0)

    def third_recv(j, total):
        frm = lax.rem(hi_i + hi - j, hi)
        third(j, frm).wait_recv()
        return total + joined(got3[frm])

    total = lax.fori_loop(
        1, hi, third_recv, acc3[hi_i])
    row = lax.broadcasted_iota(I32, (LANES, width), 0)
    col = lax.broadcasted_iota(I32, (LANES, width), 1)
    expand = jnp.where((row == col // SUB), 1.0, 0.0).astype(BF)
    inv = 1.0 / jnp.maximum(total[:, width:], 1.0)
    wide = jnp.zeros((heldp, width), F32)
    for _ in range(3):
        top = inv.astype(BF)
        wide = wide + jnp.dot(top, expand, preferred_element_type=F32)
        inv = inv - top.astype(F32)
    code_out[...] = (total[:, :width] * wide)[:held]

    row_recv()
    flat_at = lax.broadcasted_iota(I32, (rb, rblk * qc), 1)

    def unpack(i, carry):
        flat = row_got[pl.ds(i * rblk, rblk)].reshape(rblk * qc, wq)
        start = pl.multiple_of(i * rb, rb)
        for q in range(cuts):
            take = jnp.where(flat_at == place(index_col, q), 1.0, 0.0).astype(BF)
            rows_out[pl.ds(start, rb), q * wq:(q + 1) * wq] = jnp.dot(
                take, flat, preferred_element_type=F32).astype(BF)
        return carry

    lax.fori_loop(0, D * capp // rb, unpack, 0)

    id_sent()
    cent_sent()
    row_sent()
    one.wait_send()
    two.wait_send()

    def third_sent(j, carry):
        third(j, hi_i).wait_send()
        return carry

    lax.fori_loop(1, hi, third_sent, 0)


def update_kernel(ids_ref, rows_ref, cent_ref, out_ref):
    blk = cent_ref.shape[0]
    n = rows_ref.shape[0]
    base = pl.program_id(0) * blk
    slot = lax.broadcasted_iota(I32, (blk, n), 0) + base
    hit = jnp.where(slot == ids_ref[0:1, :], 1.0, 0.0)
    count = jnp.sum(hit, axis=1, keepdims=True)
    sums = jnp.dot(hit.astype(BF), rows_ref[...], preferred_element_type=F32)
    cent = cent_ref[...].astype(F32)
    out_ref[...] = ((cent + sums) * (1.0 / (count + 1.0))).astype(BF)


def shards(tokens, w_in, w_out, gain, centroids, list_slot, assign, codes, list_weight):
    count, length, width = tokens.shape
    slots_dev = centroids.shape[0]
    L, S = lax.axis_size("lists"), lax.axis_size("sub")
    D = L * S
    lo = 2
    hi = L // lo
    cap = max(2, (2 * count + D - 1) // D)
    capp = up(cap, 16)
    held = CODES // D
    heldp = up(held, 16)
    padded = up(count, LANES)
    ff = w_in.shape[1]
    wtab = width + LANES

    cuts = 4 if (4 * cap) % 16 == 0 else 8
    cfg = (L, S, lo, hi, cap, capp, cuts, slots_dev, held, heldp)
    vm = pl.BlockSpec(memory_space=pltpu.VMEM)
    anyspace = pl.BlockSpec(memory_space=pl.ANY)
    n1, n2 = lo * hi * heldp, hi * heldp
    dma = pltpu.SemaphoreType.DMA
    rows, ids, codewords = pl.pallas_call(
        functools.partial(main_kernel, cfg),
        out_shape=(
            jax.ShapeDtypeStruct((D * capp, width), BF),
            jax.ShapeDtypeStruct((8, D * capp), I32),
            jax.ShapeDtypeStruct((held, width), F32),
        ),
        in_specs=[pl.BlockSpec(memory_space=pltpu.SMEM)] + [vm] * 2 + [anyspace] * 6,
        out_specs=(vm, vm, vm),
        scratch_shapes=[
            pltpu.VMEM((list_slot.shape[0] // LANES, LANES), I32),
            pltpu.VMEM((list_slot.shape[0] // LANES, LANES), F32),
            pltpu.VMEM((padded, LANES), F32),
            pltpu.VMEM((padded, LANES), F32),
            pltpu.VMEM((padded, LANES), F32),
            pltpu.VMEM((LANES, padded), F32),
            pltpu.VMEM((count * length, width), BF),
            pltpu.VMEM((width, ff), BF),
            pltpu.VMEM((ff, width), BF),
            pltpu.VMEM((slots_dev, width), BF),
            pltpu.VMEM((padded, width), BF),
            pltpu.VMEM((D, capp, LANES), I32),
            pltpu.VMEM((D, capp, LANES), I32),
            pltpu.VMEM((D, cuts * cap, width // cuts), BF),
            pltpu.VMEM((D, cuts * cap, width // cuts), BF),
            pltpu.VMEM((D, cuts * cap, width // cuts), BF),
            pltpu.VMEM((D, cuts * cap, width // cuts), BF),
            pltpu.VMEM((S * n1, wtab), F32),
            pltpu.VMEM((hi, heldp, wtab), F32),
            pltpu.VMEM((n1, wtab), F32),
            pltpu.VMEM((n2, wtab), BF),
            pltpu.VMEM((n2, wtab), BF),
            pltpu.VMEM((hi, heldp, wtab), BF),
            pltpu.VMEM((hi, heldp, wtab), BF),
            dma((16,)),
            dma((D,)), dma((D,)), dma((D,)), dma((D,)), dma((D,)), dma((D,)),
            dma((2 + hi,)), dma((2 + hi,)),
        ],
        compiler_params=pltpu.CompilerParams(
            collective_id=0, has_side_effects=True, vmem_limit_bytes=60 * 1024 * 1024),
        name="encode_route",
    )(
        assign, codes, gain.reshape(1, width),
        list_slot.reshape(-1, LANES), list_weight.reshape(-1, LANES), tokens.reshape(count * length, width), w_in, w_out, centroids,
    )

    blk = min(512, slots_dev)
    updated = pl.pallas_call(
        update_kernel,
        grid=(slots_dev // blk,),
        out_shape=jax.ShapeDtypeStruct((slots_dev, width), BF),
        in_specs=[
            pl.BlockSpec((8, D * capp), lambda i: (0, 0)),
            pl.BlockSpec((D * capp, width), lambda i: (0, 0)),
            pl.BlockSpec((blk, width), lambda i: (i, 0)),
        ],
        out_specs=pl.BlockSpec((blk, width), lambda i: (i, 0)),
        compiler_params=pltpu.CompilerParams(vmem_limit_bytes=62 * 1024 * 1024),
        name="update_lists",
    )(ids, rows, centroids)
    return updated, codewords


def solution(mesh):
    return jax.shard_map(
        shards,
        mesh=mesh,
        in_specs=(
            P(("groups", "lists", "sub"), None, None),
            P(),
            P(),
            P(),
            P(("lists", "sub"), None),
            P("groups"),
            P(("groups", "lists", "sub")),
            P(("groups", "lists", "sub"), None),
            P("groups"),
        ),
        out_specs=(P(("groups", "lists", "sub"), None), P(("groups", "lists", "sub"), None)),
        check_vma=False,
    )
```

```python
import functools

import jax
import jax.numpy as jnp
from jax import lax
from jax.experimental import pallas as pl
from jax.experimental.pallas import tpu as pltpu
from jax.sharding import PartitionSpec as P

CODES = 256
LANES = 128
SUB = 16
BF, F32, I32 = jnp.bfloat16, jnp.float32, jnp.int32
MESH = pl.DeviceIdType.MESH


def up(value, step):
    return (value + step - 1) // step * step


def gelu(x):
    inner = x * (0.7978845608028654 + 0.035677408136300125 * (x * x))
    return 0.5 * x * (1.0 + jnp.tanh(inner))


def main_kernel(
    cfg,
    assign_ref, codes_in, gain_ref, slot_hbm, weight_hbm,
    tok_hbm, win_hbm, wout_hbm, cent_hbm,
    rows_out, ids_out, code_out,
    slot_tab, weight_tab, slot_hit, weight_hit, codes_ref,
    tok, win, wout, cent, pooled,
    ids_send, ids_got, cent_send, cent_got, row_send, row_got,
    table, acc3, got1, send2, got2, send3, got3,
    load_sem, id_s, id_r, cent_s, cent_r, row_s, row_r, t_s, t_r,
):
    L, S, lo, hi, cap, capp, cuts, slots_dev, held, heldp = cfg
    D = L * S
    width = tok.shape[1]
    wq, qc = width // cuts, cuts * cap
    passages = tok.shape[0] // 8
    padded = slot_hit.shape[0]
    li, si = lax.axis_index("lists"), lax.axis_index("sub")
    me = li * S + si
    hi_i, lo_i = li // lo, lax.rem(li, lo)
    ff = win.shape[1]
    nchunk = 4
    fc = ff // nchunk

    def dev(index):
        return {"lists": index // S, "sub": lax.rem(index, S)}

    loads = [pltpu.make_async_copy(tok_hbm, tok, load_sem.at[0])]
    for c in range(nchunk):
        loads.append(pltpu.make_async_copy(
            win_hbm.at[:, pl.ds(c * fc, fc)], win.at[:, pl.ds(c * fc, fc)], load_sem.at[1 + 2 * c]))
        loads.append(pltpu.make_async_copy(
            wout_hbm.at[pl.ds(c * fc, fc), :], wout.at[pl.ds(c * fc, fc), :], load_sem.at[2 + 2 * c]))
    cent_load = pltpu.make_async_copy(cent_hbm, cent, load_sem.at[1 + 2 * nchunk])
    slot_load = pltpu.make_async_copy(slot_hbm, slot_tab, load_sem.at[2 + 2 * nchunk])
    weight_load = pltpu.make_async_copy(weight_hbm, weight_tab, load_sem.at[3 + 2 * nchunk])
    slot_load.start()
    weight_load.start()
    cent_load.start()
    for one in loads:
        one.start()

    barrier = pltpu.get_barrier_semaphore()

    def greet(j, carry):
        pl.semaphore_signal(barrier, inc=1, device_id=dev(lax.rem(me + j, D)), device_id_type=MESH)
        return carry

    lax.fori_loop(1, D, greet, 0)

    shift = slots_dev.bit_length() - 1
    slot_hit[...] = jnp.zeros_like(slot_hit)
    weight_hit[...] = jnp.zeros_like(weight_hit)
    lane1 = lax.broadcasted_iota(I32, (1, LANES), 1)
    slot_load.wait()
    weight_load.wait()

    def look(p, carry):
        a = assign_ref[p]
        row = lax.shift_right_logical(a, 7)
        at = lane1 == jnp.bitwise_and(a, LANES - 1)
        slot_hit[pl.ds(p, 1), :] = jnp.where(at, slot_tab[pl.ds(row, 1), :].astype(F32), 0.0)
        weight_hit[pl.ds(p, 1), :] = jnp.where(at, weight_tab[pl.ds(row, 1), :], 0.0)
        return carry

    lax.fori_loop(0, passages, look, 0, unroll=8)
    below = lax.broadcasted_iota(I32, (padded, 1), 0) < passages
    slot_f = jnp.where(below, jnp.sum(slot_hit[...], axis=1, keepdims=True), -1.0)
    slot_col = slot_f.astype(I32)
    i0 = lax.broadcasted_iota(I32, (padded, padded), 0)
    i1 = lax.broadcasted_iota(I32, (padded, padded), 1)
    slot_row = jnp.sum(jnp.where(i0 == i1, slot_f, 0.0), axis=0, keepdims=True).astype(I32)
    tr = jnp.where(slot_row >= 0, lax.shift_right_logical(slot_row, shift), -1)
    tc = jnp.where(slot_col >= 0, lax.shift_right_logical(slot_col, shift), -1)
    same = tr == tc
    rank_row = jnp.sum(jnp.where(same & (i0 < i1), 1.0, 0.0), axis=0, keepdims=True).astype(I32)
    rank_col = jnp.sum(jnp.where(same & (i1 < i0), 1.0, 0.0), axis=1, keepdims=True).astype(I32)
    dest_row = jnp.where(tr >= 0, tr * capp + rank_row, -1)
    packed_row = jnp.where(tr >= 0, tr * qc + rank_row, -(1 << 20))
    packed_col = jnp.where(tc >= 0, tc * qc + rank_col, -(1 << 20))
    local_row = (slot_row - jnp.maximum(tr, 0) * slots_dev + 1).astype(F32)
    di = lax.broadcasted_iota(I32, (D * capp, padded), 0)
    spread = di == dest_row
    ids = jnp.sum(jnp.where(spread, local_row, 0.0), axis=1, keepdims=True).astype(I32) - 1
    ids_send[...] = jnp.broadcast_to(ids, (D * capp, LANES)).reshape(D, capp, LANES)
    ids_got[me] = ids_send[me]

    pl.semaphore_wait(barrier, D - 1)

    def exchange(send, got, ss, rs):
        def start(j, carry):
            to = lax.rem(me + j, D)
            pltpu.make_async_remote_copy(
                src_ref=send.at[to], dst_ref=got.at[me], send_sem=ss.at[j], recv_sem=rs.at[j],
                device_id=dev(to), device_id_type=MESH).start()
            return carry

        lax.fori_loop(1, D, start, 0)

        def finish_recv():
            def body(j, carry):
                frm = lax.rem(me + D - j, D)
                pltpu.make_async_remote_copy(
                    src_ref=send.at[frm], dst_ref=got.at[frm], send_sem=ss.at[j],
                    recv_sem=rs.at[j], device_id=dev(frm), device_id_type=MESH).wait_recv()
                return carry
            lax.fori_loop(1, D, body, 0)

        def finish_send():
            def body(j, carry):
                to = lax.rem(me + j, D)
                pltpu.make_async_remote_copy(
                    src_ref=send.at[to], dst_ref=got.at[me], send_sem=ss.at[j],
                    recv_sem=rs.at[j], device_id=dev(to), device_id_type=MESH).wait_send()
                return carry
            lax.fori_loop(1, D, body, 0)

        return finish_recv, finish_send

    id_recv, id_sent = exchange(ids_send, ids_got, id_s, id_r)

    nblk = 3 if passages % 48 == 0 else 1
    per = passages // nblk
    toks = per * 8

    def encode(b, wait):
        x = tok[pl.ds(b * toks, toks), :]
        acc = x.astype(F32)
        for c in range(nchunk):
            if wait:
                loads[1 + 2 * c].wait()
            h = gelu(jnp.dot(x, win[:, c * fc:(c + 1) * fc], preferred_element_type=F32)).astype(BF)
            if wait:
                loads[2 + 2 * c].wait()
            acc = acc + jnp.dot(h, wout[c * fc:(c + 1) * fc, :], preferred_element_type=F32)
        centre = acc - jnp.mean(acc, axis=-1, keepdims=True)
        var = jnp.mean(centre * centre, axis=-1, keepdims=True)
        normed = centre * lax.rsqrt(var + 1e-05)
        avg = jnp.mean(normed.reshape(per, 8, width), axis=1) * gain_ref[...]
        scale = lax.rsqrt(jnp.mean(avg * avg, axis=-1, keepdims=True) + 1e-06)
        pooled[pl.ds(b * per, per), :] = (avg * scale).astype(BF)

    id_recv()
    cent_load.wait()
    want = ids_got[...].reshape(D * capp, LANES)
    ids_out[...] = want.T[0:8, :]
    rb = 256
    rblk = rb // capp
    cbits = capp.bit_length() - 1

    def stacked(rows):
        return jnp.concatenate([rows[:, q * wq:(q + 1) * wq] for q in range(cuts)], axis=0)

    def place(index, q):
        r = jnp.bitwise_and(index, capp - 1)
        d = lax.shift_right_logical(index, cbits)
        return jnp.where(r < cap, d * qc + q * cap + r, -1)

    index_row = lax.broadcasted_iota(I32, (1, rb), 1)
    index_col = lax.broadcasted_iota(I32, (rb, 1), 0)
    pack = jnp.concatenate([place(index_row, q) for q in range(cuts)], axis=1)
    pack = jnp.where(lax.broadcasted_iota(I32, (rblk * qc, cuts * rb), 0) == pack, 1.0, 0.0).astype(BF)

    def pick(i, carry):
        mine = ids_got[pl.ds(i * rblk, rblk)].reshape(rb, LANES)[:, 0:1]
        hit = jnp.where(lax.broadcasted_iota(I32, (rb, slots_dev), 1) == mine, 1.0, 0.0).astype(BF)
        out = jnp.dot(hit, cent[...], preferred_element_type=F32).astype(BF)
        out = jnp.dot(pack, stacked(out), preferred_element_type=F32).astype(BF)
        cent_send[pl.ds(i * rblk, rblk)] = out.reshape(rblk, qc, wq)
        return carry

    lax.fori_loop(0, D * capp // rb, pick, 0)
    cent_got[me] = cent_send[me]
    cent_recv, cent_sent = exchange(cent_send, cent_got, cent_s, cent_r)

    codes_ref[...] = jnp.full(codes_ref.shape, -1.0, F32)
    codes_ref[0:codes_in.shape[0], 0:passages] = codes_in[...].astype(F32)

    pooled[...] = jnp.zeros_like(pooled)
    loads[0].wait()
    for b in range(nblk):
        encode(b, b == 0)

    put = jnp.concatenate([packed_row + q * cap for q in range(cuts)], axis=1)
    put = jnp.where(
        lax.broadcasted_iota(I32, (D * qc, cuts * padded), 0) == put, 1.0, 0.0).astype(BF)
    row_send[...] = jnp.dot(
        put, stacked(pooled[...]), preferred_element_type=F32).astype(BF).reshape(D, qc, wq)
    row_got[me] = row_send[me]
    row_recv, row_sent = exchange(row_send, row_got, row_s, row_r)

    cent_recv()
    got_flat = cent_got[...].reshape(D * qc, wq)
    get_at = lax.broadcasted_iota(I32, (padded, D * qc), 1)
    cent_rows = jnp.concatenate([
        jnp.dot(jnp.where(get_at == packed_col + q * cap, 1.0, 0.0).astype(BF), got_flat,
                preferred_element_type=F32) for q in range(cuts)], axis=1)
    weight = jnp.sum(weight_hit[...], axis=1, keepdims=True)
    resid = (pooled[...].astype(F32) - cent_rows) * weight
    r_hi = resid.astype(BF).astype(F32)
    r_lo = resid - r_hi
    w_hi = weight.astype(BF).astype(F32)
    w_lo = weight - w_hi

    nrow = S * lo * hi * heldp
    tb = 256
    lane = lax.broadcasted_iota(I32, (padded, LANES), 1)
    group = LANES // SUB
    ngroup = width // LANES
    logical = {"hp": heldp.bit_length() - 1}

    def build(i, carry):
        t = lax.broadcasted_iota(I32, (tb, 1), 0) + i * tb
        k = jnp.bitwise_and(t, heldp - 1)
        rest = lax.shift_right_logical(t, logical["hp"])
        h = jnp.bitwise_and(rest, hi - 1)
        rest = lax.shift_right_logical(rest, hi.bit_length() - 1)
        l = jnp.bitwise_and(rest, lo - 1)
        s = lax.shift_right_logical(rest, lo.bit_length() - 1)
        code = jnp.where(k < held, ((h * lo + l) * S + s) * held + k, -2).astype(F32)
        counts = jnp.zeros((tb, LANES), F32)
        start = pl.multiple_of(i * tb, tb)
        for j in range(ngroup):
            lhs, rhs = [], []
            part_hi = r_hi[:, j * LANES:(j + 1) * LANES]
            part_lo = r_lo[:, j * LANES:(j + 1) * LANES]
            for mm in range(group):
                m = j * group + mm
                lhs.append(jnp.where(codes_ref[m:m + 1, :] == code, 1.0, 0.0).astype(BF))
                own = lane // SUB == mm
                data = jnp.where(own, part_hi, 0.0).astype(BF)
                rest_data = jnp.where(own, part_lo, 0.0).astype(BF)
                cnt = jnp.where(lane == m, w_hi, jnp.where(lane == 64 + m, w_lo, 0.0)).astype(BF)
                rhs.append(jnp.concatenate([data, rest_data, cnt], axis=1))
            out = jnp.dot(jnp.concatenate(lhs, axis=1), jnp.concatenate(rhs, axis=0),
                          preferred_element_type=F32)
            table[pl.ds(start, tb), j * LANES:(j + 1) * LANES] = (
                out[:, :LANES] + out[:, LANES:2 * LANES])
            counts = counts + out[:, 2 * LANES:]
        total = counts + pltpu.roll(counts, 64, 1)
        table[pl.ds(start, tb), width:] = total
        return carry

    def split(total):
        first = total.astype(BF)
        keep = lax.broadcasted_iota(I32, total.shape, 1) < 64
        return jnp.where(keep, first.astype(F32), total - first.astype(F32)).astype(BF)

    def joined(block):
        wide = block.astype(F32)
        tail = wide[:, width:]
        return jnp.concatenate([wide[:, :width], tail + pltpu.roll(tail, 64, 1)], axis=1)

    def narrow(block):
        return jnp.concatenate([block[:, :width].astype(BF), split(block[:, width:])], axis=1)

    lax.fori_loop(0, nrow // tb, build, 0)

    n1, n2 = lo * hi * heldp, hi * heldp

    def swap(src, dst, at, device):
        return pltpu.make_async_remote_copy(
            src_ref=src, dst_ref=dst, send_sem=t_s.at[at], recv_sem=t_r.at[at],
            device_id=device, device_id_type=MESH)

    other = 1 - si
    one = swap(table.at[pl.ds(pl.multiple_of(other * n1, 16), n1)], got1, 0, {"lists": li, "sub": other})
    one.start()
    one.wait_recv()
    lo_o = 1 - lo_i
    mine1 = pl.multiple_of(si * n1, 16)
    away = pl.multiple_of(lo_o * n2, 16)
    near = pl.multiple_of(lo_i * n2, 16)
    send2[...] = narrow(table[pl.ds(mine1 + away, n2), :] + got1[pl.ds(away, n2), :])
    two = swap(send2, got2, 1, {"lists": hi_i * lo + lo_o, "sub": si})
    two.start()
    acc = table[pl.ds(mine1 + near, n2), :] + got1[pl.ds(near, n2), :]
    two.wait_recv()
    acc = acc + joined(got2[...])
    acc3[...] = acc.reshape(hi, heldp, width + LANES)
    send3[...] = narrow(acc).reshape(hi, heldp, width + LANES)

    def third(j, frm):
        return pltpu.make_async_remote_copy(
            src_ref=send3.at[lax.rem(hi_i + j, hi)], dst_ref=got3.at[frm],
            send_sem=t_s.at[2 + j], recv_sem=t_r.at[2 + j],
            device_id={"lists": lax.rem(hi_i + j, hi) * lo + lo_i, "sub": si}, device_id_type=MESH)

    def third_start(j, carry):
        third(j, hi_i).start()
        return carry

    lax.fori_loop(1, hi, third_start, 0)

    def third_recv(j, total):
        frm = lax.rem(hi_i + hi - j, hi)
        third(j, frm).wait_recv()
        return total + joined(got3[frm])

    total = lax.fori_loop(
        1, hi, third_recv, acc3[hi_i])
    row = lax.broadcasted_iota(I32, (LANES, width), 0)
    col = lax.broadcasted_iota(I32, (LANES, width), 1)
    expand = jnp.where((row == col // SUB), 1.0, 0.0).astype(BF)
    inv = 1.0 / jnp.maximum(total[:, width:], 1.0)
    wide = jnp.zeros((heldp, width), F32)
    for _ in range(3):
        top = inv.astype(BF)
        wide = wide + jnp.dot(top, expand, preferred_element_type=F32)
        inv = inv - top.astype(F32)
    code_out[...] = (total[:, :width] * wide)[:held]

    row_recv()
    flat_at = lax.broadcasted_iota(I32, (rb, rblk * qc), 1)

    def unpack(i, carry):
        flat = row_got[pl.ds(i * rblk, rblk)].reshape(rblk * qc, wq)
        start = pl.multiple_of(i * rb, rb)
        for q in range(cuts):
            take = jnp.where(flat_at == place(index_col, q), 1.0, 0.0).astype(BF)
            rows_out[pl.ds(start, rb), q * wq:(q + 1) * wq] = jnp.dot(
                take, flat, preferred_element_type=F32).astype(BF)
        return carry

    lax.fori_loop(0, D * capp // rb, unpack, 0)

    id_sent()
    cent_sent()
    row_sent()
    one.wait_send()
    two.wait_send()

    def third_sent(j, carry):
        third(j, hi_i).wait_send()
        return carry

    lax.fori_loop(1, hi, third_sent, 0)


def update_kernel(ids_ref, rows_ref, cent_ref, out_ref):
    blk = cent_ref.shape[0]
    n = rows_ref.shape[0]
    base = pl.program_id(0) * blk
    slot = lax.broadcasted_iota(I32, (blk, n), 0) + base
    hit = jnp.where(slot == ids_ref[0:1, :], 1.0, 0.0)
    count = jnp.sum(hit, axis=1, keepdims=True)
    sums = jnp.dot(hit.astype(BF), rows_ref[...], preferred_element_type=F32)
    cent = cent_ref[...].astype(F32)
    out_ref[...] = ((cent + sums) * (1.0 / (count + 1.0))).astype(BF)


def shards(tokens, w_in, w_out, gain, centroids, list_slot, assign, codes, list_weight):
    count, length, width = tokens.shape
    slots_dev = centroids.shape[0]
    L, S = lax.axis_size("lists"), lax.axis_size("sub")
    D = L * S
    lo = 2
    hi = L // lo
    cap = max(2, (2 * count + D - 1) // D)
    capp = up(cap, 16)
    held = CODES // D
    heldp = up(held, 16)
    padded = up(count, LANES)
    ff = w_in.shape[1]
    wtab = width + LANES

    cuts = 4 if (4 * cap) % 16 == 0 else 8
    cfg = (L, S, lo, hi, cap, capp, cuts, slots_dev, held, heldp)
    vm = pl.BlockSpec(memory_space=pltpu.VMEM)
    anyspace = pl.BlockSpec(memory_space=pl.ANY)
    n1, n2 = lo * hi * heldp, hi * heldp
    dma = pltpu.SemaphoreType.DMA
    rows, ids, codewords = pl.pallas_call(
        functools.partial(main_kernel, cfg),
        out_shape=(
            jax.ShapeDtypeStruct((D * capp, width), BF),
            jax.ShapeDtypeStruct((8, D * capp), I32),
            jax.ShapeDtypeStruct((held, width), F32),
        ),
        in_specs=[pl.BlockSpec(memory_space=pltpu.SMEM)] + [vm] * 2 + [anyspace] * 6,
        out_specs=(vm, vm, vm),
        scratch_shapes=[
            pltpu.VMEM((list_slot.shape[0] // LANES, LANES), I32),
            pltpu.VMEM((list_slot.shape[0] // LANES, LANES), F32),
            pltpu.VMEM((padded, LANES), F32),
            pltpu.VMEM((padded, LANES), F32),
            pltpu.VMEM((LANES, padded), F32),
            pltpu.VMEM((count * length, width), BF),
            pltpu.VMEM((width, ff), BF),
            pltpu.VMEM((ff, width), BF),
            pltpu.VMEM((slots_dev, width), BF),
            pltpu.VMEM((padded, width), BF),
            pltpu.VMEM((D, capp, LANES), I32),
            pltpu.VMEM((D, capp, LANES), I32),
            pltpu.VMEM((D, cuts * cap, width // cuts), BF),
            pltpu.VMEM((D, cuts * cap, width // cuts), BF),
            pltpu.VMEM((D, cuts * cap, width // cuts), BF),
            pltpu.VMEM((D, cuts * cap, width // cuts), BF),
            pltpu.VMEM((S * n1, wtab), F32),
            pltpu.VMEM((hi, heldp, wtab), F32),
            pltpu.VMEM((n1, wtab), F32),
            pltpu.VMEM((n2, wtab), BF),
            pltpu.VMEM((n2, wtab), BF),
            pltpu.VMEM((hi, heldp, wtab), BF),
            pltpu.VMEM((hi, heldp, wtab), BF),
            dma((16,)),
            dma((D,)), dma((D,)), dma((D,)), dma((D,)), dma((D,)), dma((D,)),
            dma((2 + hi,)), dma((2 + hi,)),
        ],
        compiler_params=pltpu.CompilerParams(
            collective_id=0, has_side_effects=True, vmem_limit_bytes=60 * 1024 * 1024),
        name="encode_route",
    )(
        assign, codes.T, gain.reshape(1, width),
        list_slot.reshape(-1, LANES), list_weight.reshape(-1, LANES), tokens.reshape(count * length, width), w_in, w_out, centroids,
    )

    blk = min(256, slots_dev)
    updated = pl.pallas_call(
        update_kernel,
        grid=(slots_dev // blk,),
        out_shape=jax.ShapeDtypeStruct((slots_dev, width), BF),
        in_specs=[
            pl.BlockSpec((8, D * capp), lambda i: (0, 0)),
            pl.BlockSpec((D * capp, width), lambda i: (0, 0)),
            pl.BlockSpec((blk, width), lambda i: (i, 0)),
        ],
        out_specs=pl.BlockSpec((blk, width), lambda i: (i, 0)),
        compiler_params=pltpu.CompilerParams(vmem_limit_bytes=62 * 1024 * 1024),
        name="update_lists",
    )(ids, rows, centroids)
    return updated, codewords


def solution(mesh):
    return jax.shard_map(
        shards,
        mesh=mesh,
        in_specs=(
            P(("groups", "lists", "sub"), None, None),
            P(),
            P(),
            P(),
            P(("lists", "sub"), None),
            P("groups"),
            P(("groups", "lists", "sub")),
            P(("groups", "lists", "sub"), None),
            P("groups"),
        ),
        out_specs=(P(("groups", "lists", "sub"), None), P(("groups", "lists", "sub"), None)),
        check_vma=False,
    )
```
